512 devices in a mesh: hist: 256 (over z, x, y_lo, core), orb: 2 (over y_hi).
Axes of the slice: x: 4, y: 4 (y_hi: 2, y_lo: 2; y = y_hi * 2 + y_lo), z: 16, core: 2. Of those that a mesh axis runs over, the one named last changes fastest.
Arguments:
- g_hist: bfloat16 [512, 64, 32768], P('hist', 'orb'), may hold values from -6 to 6
- sigma_hist: bfloat16 [2, 64, 32768], P(None, None, 'hist'), may hold values from -0.03125 to 0.03125
- diag_inv: float32 [512, 64, 64], P('hist'), may hold values from -0.75 to 0.75
- previous: float32 [2, 512, 64, 64], P(None, 'hist', 'orb'), may hold values from -6 to 6
- block_of_slot: int32 [256], replicated, may hold values from 0 to 255, each once
- front_pos: int32 [2], replicated, may hold values from 256 to 511
Outputs:
- g_row: float32 [2, 512, 64, 64], P(None, 'hist', 'orb')
- sigma_row: float32 [2, 512, 64, 64], P(None, 'hist', 'orb')
The draws below stay inside these ranges and needn't reach their ends.
Inputs may be any that keep to these rules, and one draw needn't show every extreme that they name: `block_of_slot`: every block index appears once.
All inputs are finite; a program needn't handle non-finite values.
Results may differ from the reference program's by a relative error of at most 0.0003.
Values may be sent and summed in bfloat16 or wider, within the bound.
No kernel may reach another device: no remote copies, remote signals or barrier semaphores. Data moves between devices by JAX's collectives and lax.ppermute only.
A program may use at most 64 MiB of HBM per device.

```python
import jax
import jax.numpy as jnp
from jax import lax

O = 64
TB = 2
NT = 512
N_HIST = 256


def shard_levels(own_key, dims, split, low, largest):
    level = 1.0
    for axis_at, blocks in split:
        steps = jax.random.uniform(jax.random.fold_in(jax.random.fold_in(own_key, 6), axis_at), (blocks,), jnp.float32, low / len(split), largest / len(split))
        level = level * jnp.repeat(jnp.exp(steps), dims[axis_at] // blocks).reshape((-1,) + (1,) * (len(dims) - 1 - axis_at))
    return level


def noise(own_key, dims, spread, bound, shards=(), held_as=jnp.bfloat16):
    gain = shard_levels(own_key, dims, shards, -0.22, 0.18) if shards else 1.0
    values = jax.random.normal(own_key, dims, jnp.float32) * spread * gain
    return jnp.minimum(jnp.maximum(values, -bound), bound).astype(held_as)


def setup_inputs(seed: int = 0) -> dict:
    key_list = jax.random.split(jax.random.key(seed), 7)
    return {
        "g_hist": noise(key_list[0], (NT, O, NT * O), 1.0, 6.0, ((0, 256), (1, 2))),
        "sigma_hist": noise(key_list[1], (2, O, NT * O), (NT * O) ** -0.5, 0.03125, ((2, 256),)),
        "diag_inv": noise(key_list[2], (NT, O, O), O ** -0.5, 0.75, ((0, 256),), jnp.float32),
        "previous": noise(key_list[3], (2, NT, O, O), 1.0, 6.0, ((1, 256), (2, 2)), jnp.float32),
        "block_of_slot": jax.random.permutation(key_list[4], N_HIST).astype(jnp.int32),
        "front_pos": jax.random.randint(key_list[5], (2,), NT // 2, NT).astype(jnp.int32),
    }


COUPLING = 0.5


def reference(g_hist, sigma_hist, diag_inv, previous, block_of_slot, front_pos):
    slot_rows = jnp.arange(NT, dtype=jnp.int32)
    col_time = (block_of_slot[slot_rows // TB] * TB + slot_rows % TB).astype(jnp.int32)
    times = (jnp.arange(NT * O, dtype=jnp.int32) // O).astype(jnp.int32)
    front_keep = times[None, :] <= front_pos[:, None]
    sigma_kept = jnp.where(front_keep[:, None, :], sigma_hist, jnp.zeros_like(sigma_hist)).astype(jnp.float32)

    def column(item):
        g_one, when = item
        g_kept = jnp.where((times >= when)[None, :], g_one, jnp.zeros_like(g_one)).astype(jnp.float32)
        return jnp.einsum("cx,fax->fca", g_kept, sigma_kept)

    integral = lax.map(column, (g_hist, col_time))
    integral = jnp.transpose(integral, (1, 0, 2, 3))
    combined = previous + integral
    rows = diag_inv[front_pos]
    g_row = jnp.einsum("ftcb,fab->ftca", combined, rows, precision=lax.Precision.HIGHEST)
    sigma_row = COUPLING * g_row * g_row * jnp.swapaxes(g_row, 2, 3)
    return g_row, sigma_row
```

```python
import jax
import jax.numpy as jnp
from jax import lax
from jax.experimental import pallas as pl
from jax.experimental.pallas import tpu as pltpu
from jax.sharding import Mesh
from jax.sharding import PartitionSpec as P

HIST = ("z", "x", "yl", "core")
RING = ("yl", "yh")
COUPLING = 0.5
SPLIT_ROWS = 32
F32 = jnp.float32
BF16 = jnp.bfloat16
VMEM = pltpu.VMEM
SMEM = pltpu.SMEM


def whole(space=VMEM):
    return pl.BlockSpec(memory_space=space)


def ring_index(y):
    return (y % 2) * 2 + y // 2


def prep_kernel(slots, fronts, g_ref, sigma_ref, inv_ref, *outs):
    piece_refs, share_ref, chunk_ref = outs[:4], outs[4], outs[5]
    pair = pl.program_id(0)
    yl, core, yh = lax.axis_index("yl"), lax.axis_index("core"), lax.axis_index("yh")
    hist = ((lax.axis_index("z") * 4 + lax.axis_index("x")) * 2 + yl) * 2 + core
    first = slots[hist] * 2
    lane = lax.broadcasted_iota(jnp.int32, (64, 128), 1)
    row = lax.broadcasted_iota(jnp.int32, (64, 128), 0)
    upper = (lane >= 64).astype(jnp.int32)
    ahead = pair * 64 + upper * 32 - first - (row >= 32).astype(jnp.int32)
    pick_in = lax.broadcasted_iota(jnp.int32, (256, 128), 0)
    pick_out = lax.broadcasted_iota(jnp.int32, (256, 128), 1)
    pick_out = pick_out + 64 * (pick_out >= 64).astype(jnp.int32)
    for d in range(4):
        y = (yh * 2 + yl + d) % 4
        to_yl, to_yh = y % 2, y // 2
        pick = jnp.where(pick_in == pick_out + 64 * to_yh, 1.0, 0.0).astype(BF16)
        blocks = []
        for h in range(2):
            to_core = core if h == 0 else 1 - core
            for x in range(4):
                at = (x * 4 + to_yl * 2 + to_core) * 128
                even = g_ref[:, pl.ds(pl.multiple_of(at, 128), 128)]
                odd = g_ref[:, pl.ds(pl.multiple_of(at + 2048, 128), 128)]
                blocks.append(jnp.concatenate([even, odd], axis=1))
        picked = jnp.dot(jnp.concatenate(blocks, axis=0), pick, preferred_element_type=F32)
        for h in range(2):
            to_core = core if h == 0 else 1 - core
            for x in range(4):
                at = h * 4 + x
                term = x * 8 + to_yl * 4 + to_core * 2 + to_yh
                kept = jnp.where(ahead + term >= 0, picked[at * 64 : at * 64 + 64], 0.0)
                piece_refs[d][at] = kept.astype(BF16)

    @pl.when(pair == 0)
    def _():
        flipped = sigma_ref[...].astype(F32).T
        mine = jnp.where(yh == 0, flipped[:64], flipped[64:])
        limit = jnp.where(upper > 0, fronts[1], fronts[0])
        chunk_ref[...] = jnp.where(2 * hist + yh <= limit, mine, 0.0).astype(BF16)
        when = jnp.where(yh == 0, fronts[0], fronts[1])
        block = jnp.where(when % 2 == 0, inv_ref[0], inv_ref[1])
        block = jnp.where(when // 2 == hist, block, 0.0)
        share_ref[:, :64] = block[:32]
        share_ref[:, 64:] = block[32:]


def prep(slots, fronts, g_hist, sigma_hist, diag_inv):
    return pl.pallas_call(
        prep_kernel,
        grid=(8,),
        in_specs=[
            whole(SMEM),
            whole(SMEM),
            pl.BlockSpec((64, 4096), lambda i: (0, i)),
            pl.BlockSpec((128, 128), lambda i: (0, 0)),
            pl.BlockSpec((2, 64, 64), lambda i: (0, 0, 0)),
        ],
        out_specs=[pl.BlockSpec((8, 64, 128), lambda i: (0, 0, i))] * 4
        + [pl.BlockSpec((32, 128), lambda i: (0, 0)), pl.BlockSpec((64, 128), lambda i: (0, 0))],
        out_shape=[jax.ShapeDtypeStruct((8, 64, 1024), BF16)] * 4
        + [jax.ShapeDtypeStruct((32, 128), F32), jax.ShapeDtypeStruct((64, 128), BF16)],
        name="prep",
    )(slots, fronts, g_hist, sigma_hist, diag_inv)


def along_z_kernel(shares_ref, chunk_ref, out_ref):
    core = lax.axis_index("core")
    share = shares_ref[0] + shares_ref[1]
    mine = jnp.where(core == 0, share[:16], share[16:])
    high = mine.astype(BF16)
    low = (mine - high.astype(F32)).astype(BF16)
    message = jnp.concatenate([chunk_ref[...], high, low], axis=0)
    for z in range(16):
        out_ref[z] = message


def along_x_kernel(in_ref, out_ref):
    share = in_ref[0, 64:].astype(F32)
    for z in range(1, 16):
        share = share + in_ref[z, 64:].astype(F32)
    share = share.astype(BF16)
    for x in range(4):
        for z in range(16):
            out_ref[x, z * 64 : z * 64 + 64] = in_ref[z, :64]
        out_ref[x, 1024:] = share


def first_kernel(s_ref, g0, g1, g2, g3, out_ref):
    rows = jnp.concatenate([g0[0], g1[0], g2[0], g3[0]], axis=0)
    part = jnp.dot(rows, s_ref[0, :1024], preferred_element_type=F32)

    @pl.when(pl.program_id(0) == 0)
    def _():
        out_ref[...] = part

    @pl.when(pl.program_id(0) > 0)
    def _():
        out_ref[...] += part


def second_kernel(s_ref, g0, g1, g2, g3, part_ref, mine_ref, other_ref, prev_ref, out_ref, total):
    rows = jnp.concatenate([g0[0], g1[0], g2[0], g3[0]], axis=0)
    part = jnp.dot(rows, s_ref[0, :1024], preferred_element_type=F32).reshape(4, 64, 128)
    step = pl.program_id(0)

    @pl.when(step == 0)
    def _():
        total[...] = part + part_ref[...]

    @pl.when(step > 0)
    def _():
        total[...] += part

    @pl.when(step == 3)
    def _():
        core, yl, yh = lax.axis_index("core"), lax.axis_index("yl"), lax.axis_index("yh")
        before = [prev_ref[f].reshape(64, 64) for f in range(2)]
        total[0] += jnp.concatenate(before, axis=1)

        def joined(ref):
            halves = ref[...].astype(F32)
            halves = halves[0] + halves[1] + halves[2] + halves[3]
            return halves[:16] + halves[16:]

        mine, other = joined(mine_ref), joined(other_ref)
        share = jnp.concatenate(
            [jnp.where(core == 0, mine, other), jnp.where(core == 0, other, mine)], axis=0
        )
        for to in range(4):
            for half in range(2):
                d = (yh * 2 + yl + 4 - (half * 2 + to // 2)) % 4
                out_ref[to, half * 64 : half * 64 + 64] = total[d]
            out_ref[to, 128:] = share


def dots(s, pieces, half, extra=(), extra_specs=(), kernel=first_kernel, out=(256, 128), scratch=()):
    return pl.pallas_call(
        kernel,
        grid=(4,),
        in_specs=[pl.BlockSpec((1, 1056, 128), lambda i: (i, 0, 0))]
        + [pl.BlockSpec((1, 64, 1024), lambda i: (half * 4 + i, 0, 0))] * 4
        + list(extra_specs),
        out_specs=pl.BlockSpec(out, lambda i: (0,) * len(out)),
        out_shape=jax.ShapeDtypeStruct(out, F32),
        scratch_shapes=list(scratch),
        cost_estimate=pl.CostEstimate(
            flops=2 * 256 * 4096 * 128, bytes_accessed=3 << 20, transcendentals=0
        ),
        name=kernel.__name__,
    )(s, *pieces, *extra)


def last_kernel(in_ref, g_ref, s_ref):
    yh = lax.axis_index("yh")
    combined = in_ref[0, :128] + in_ref[1, :128] + in_ref[2, :128] + in_ref[3, :128]
    for f in range(2):
        share = in_ref[f, 128:] + in_ref[2 + f, 128:]
        rows = jnp.concatenate([share[:, :64], share[:, 64:]], axis=0)
        g = lax.dot_general(
            combined[:, f * 64 : f * 64 + 64],
            rows,
            (((1,), (1,)), ((), ())),
            precision=lax.Precision.HIGHEST,
            preferred_element_type=F32,
        )
        for r in range(2):
            low, high = g[r * 32 : r * 32 + 32], g[64 + r * 32 : 96 + r * 32]
            flipped = jnp.concatenate([low, high], axis=0).T
            mirror = jnp.where(yh == 0, flipped[:32], flipped[32:])
            mine = jnp.where(yh == 0, low, high)
            g_ref[f, r] = mine
            s_ref[f, r] = COUPLING * mine * mine * mirror


def body(g_hist, sigma_hist, diag_inv, previous, block_of_slot, front_pos):
    *pieces, share, chunk = prep(
        block_of_slot,
        front_pos,
        g_hist.reshape(64, 32768),
        sigma_hist.reshape(128, 128),
        diag_inv,
    )
    rows = [pieces[0]]
    for d in (2, 1, 3):
        pairs = [(ring_index(y), ring_index((y + d) % 4)) for y in range(4)]
        rows.append(lax.ppermute(pieces[d], RING, pairs))
    rows = [rows[0], rows[2], rows[1], rows[3]]
    shares = lax.all_gather(share, "core")
    message = pl.pallas_call(
        along_z_kernel,
        in_specs=[whole(), whole()],
        out_specs=whole(),
        out_shape=jax.ShapeDtypeStruct((16, 96, 128), BF16),
        name="along_z",
    )(shares, chunk)
    message = lax.all_to_all(message, "z", 0, 0, tiled=True)
    message = pl.pallas_call(
        along_x_kernel,
        in_specs=[whole()],
        out_specs=whole(),
        out_shape=jax.ShapeDtypeStruct((4, 1056, 128), BF16),
        name="along_x",
    )(message)
    mine = lax.all_to_all(message, "x", 0, 0, tiled=True)
    other = lax.ppermute(mine, "core", [(0, 1), (1, 0)])
    part = dots(mine, rows, 0)
    tail = pl.BlockSpec((4, SPLIT_ROWS, 128), lambda i: (0, 1024 // SPLIT_ROWS, 0))
    sums = dots(
        other,
        rows,
        1,
        (part.reshape(4, 64, 128), mine, other, previous),
        (
            pl.BlockSpec((4, 64, 128), lambda i: (0, 0, 0)),
            tail,
            tail,
            pl.BlockSpec((2, 2, 32, 64), lambda i: (0, 0, 0, 0)),
        ),
        second_kernel,
        (4, 160, 128),
        (VMEM((4, 64, 128), F32),),
    )
    sums = lax.all_to_all(sums, RING, 0, 0, tiled=True)
    out = jax.ShapeDtypeStruct(previous.shape, F32)
    return pl.pallas_call(
        last_kernel,
        in_specs=[whole()],
        out_specs=(whole(), whole()),
        out_shape=(out, out),
        name="last",
    )(sums)


def solution(mesh):
    split = Mesh(mesh.devices.reshape(16, 4, 2, 2, 2), (*HIST, "yh"))
    in_specs = (
        P(HIST, "yh", None),
        P(None, None, HIST),
        P(HIST, None, None),
        P(None, HIST, "yh", None),
        P(),
        P(),
    )
    out_specs = (P(None, HIST, "yh", None), P(None, HIST, "yh", None))
    return jax.shard_map(body, mesh=split, in_specs=in_specs, out_specs=out_specs, check_vma=False)
```

```python
import jax
import jax.numpy as jnp
from jax import lax
from jax.experimental import pallas as pl
from jax.experimental.pallas import tpu as pltpu
from jax.sharding import Mesh
from jax.sharding import PartitionSpec as P

HIST = ("z", "x", "yl", "core")
RING = ("yl", "yh")
COUPLING = 0.5
PAIRS = 2
SPLIT_ROWS = 32
F32 = jnp.float32
BF16 = jnp.bfloat16
VMEM = pltpu.VMEM
SMEM = pltpu.SMEM


def whole(space=VMEM):
    return pl.BlockSpec(memory_space=space)


def ring_index(y):
    return (y % 2) * 2 + y // 2


def prep_kernel(slots, fronts, g_ref, sigma_ref, inv_ref, *outs):
    piece_refs, share_ref, chunk_ref = outs[:4], outs[4], outs[5]
    step = pl.program_id(0)
    yl, core, yh = lax.axis_index("yl"), lax.axis_index("core"), lax.axis_index("yh")
    hist = ((lax.axis_index("z") * 4 + lax.axis_index("x")) * 2 + yl) * 2 + core
    first = slots[hist] * 2
    lane = lax.broadcasted_iota(jnp.int32, (64, 128), 1)
    row = lax.broadcasted_iota(jnp.int32, (64, 128), 0)
    upper = (lane >= 64).astype(jnp.int32)
    ahead = upper * 32 - first - (row >= 32).astype(jnp.int32)
    pick_in = lax.broadcasted_iota(jnp.int32, (256, 256), 0)
    pick_out = lax.broadcasted_iota(jnp.int32, (256, 256), 1)
    for d in range(2):
        y = (yh * 2 + yl + d) % 4
        to_yl, to_yh = y % 2, y // 2
        half = jnp.where(pick_out < 128, to_yh, 1 - to_yh)
        within = pick_out % 128
        pick = pick_in == within + 64 * (within >= 64).astype(jnp.int32) + 64 * half
        pick = jnp.where(pick, 1.0, 0.0).astype(BF16)
        for p in range(PAIRS):
            blocks = []
            for h in range(2):
                to_core = core if h == 0 else 1 - core
                for x in range(4):
                    at = p * 4096 + (x * 4 + to_yl * 2 + to_core) * 128
                    even = g_ref[:, pl.ds(pl.multiple_of(at, 128), 128)]
                    odd = g_ref[:, pl.ds(pl.multiple_of(at + 2048, 128), 128)]
                    blocks.append(jnp.concatenate([even, odd], axis=1))
            picked = jnp.dot(jnp.concatenate(blocks, axis=0), pick, preferred_element_type=F32)
            for h in range(2):
                to_core = core if h == 0 else 1 - core
                for x in range(4):
                    at = h * 4 + x
                    term = (step * PAIRS + p) * 64 + x * 8 + to_yl * 4 + to_core * 2
                    for far in range(2):
                        e = 1 - to_yh if far else to_yh
                        block = picked[at * 64 : at * 64 + 64, far * 128 : far * 128 + 128]
                        block = jnp.where(ahead + (term + e) >= 0, block, 0.0)
                        piece_refs[d + 2 * far][at, :, p * 128 : p * 128 + 128] = block.astype(BF16)

    @pl.when(step == 0)
    def _():
        flipped = sigma_ref[...].astype(F32).T
        mine = jnp.where(yh == 0, flipped[:64], flipped[64:])
        limit = jnp.where(upper > 0, fronts[1], fronts[0])
        chunk_ref[...] = jnp.where(2 * hist + yh <= limit, mine, 0.0).astype(BF16)
        when = jnp.where(yh == 0, fronts[0], fronts[1])
        block = jnp.where(when % 2 == 0, inv_ref[0], inv_ref[1])
        block = jnp.where(when // 2 == hist, block, 0.0)
        share_ref[:, :64] = block[:32]
        share_ref[:, 64:] = block[32:]


def prep(slots, fronts, g_hist, sigma_hist, diag_inv):
    return pl.pallas_call(
        prep_kernel,
        grid=(8 // PAIRS,),
        in_specs=[
            whole(SMEM),
            whole(SMEM),
            pl.BlockSpec((64, 4096 * PAIRS), lambda i: (0, i)),
            pl.BlockSpec((128, 128), lambda i: (0, 0)),
            pl.BlockSpec((2, 64, 64), lambda i: (0, 0, 0)),
        ],
        out_specs=[pl.BlockSpec((8, 64, 128 * PAIRS), lambda i: (0, 0, i))] * 4
        + [pl.BlockSpec((32, 128), lambda i: (0, 0)), pl.BlockSpec((64, 128), lambda i: (0, 0))],
        out_shape=[jax.ShapeDtypeStruct((8, 64, 1024), BF16)] * 4
        + [jax.ShapeDtypeStruct((32, 128), F32), jax.ShapeDtypeStruct((64, 128), BF16)],
        name="prep",
    )(slots, fronts, g_hist, sigma_hist, diag_inv)


def along_z_kernel(shares_ref, chunk_ref, out_ref):
    core = lax.axis_index("core")
    share = shares_ref[0] + shares_ref[1]
    mine = jnp.where(core == 0, share[:16], share[16:])
    high = mine.astype(BF16)
    low = (mine - high.astype(F32)).astype(BF16)
    message = jnp.concatenate([chunk_ref[...], high, low], axis=0)
    for z in range(16):
        out_ref[z] = message


def along_x_kernel(in_ref, out_ref):
    share = in_ref[0, 64:].astype(F32)
    for z in range(1, 16):
        share = share + in_ref[z, 64:].astype(F32)
    share = share.astype(BF16)
    for x in range(4):
        for z in range(16):
            out_ref[x, z * 64 : z * 64 + 64] = in_ref[z, :64]
        out_ref[x, 1024:] = share


def first_kernel(s_ref, g0, g1, g2, g3, out_ref):
    rows = jnp.concatenate([g0[0], g1[0], g2[0], g3[0]], axis=0)
    part = jnp.dot(rows, s_ref[0, :1024], preferred_element_type=F32)

    @pl.when(pl.program_id(0) == 0)
    def _():
        out_ref[...] = part

    @pl.when(pl.program_id(0) > 0)
    def _():
        out_ref[...] += part


def second_kernel(s_ref, g0, g1, g2, g3, part_ref, mine_ref, other_ref, prev_ref, out_ref, total):
    rows = jnp.concatenate([g0[0], g1[0], g2[0], g3[0]], axis=0)
    part = jnp.dot(rows, s_ref[0, :1024], preferred_element_type=F32).reshape(4, 64, 128)
    step = pl.program_id(0)

    @pl.when(step == 0)
    def _():
        total[...] = part + part_ref[...]

    @pl.when(step > 0)
    def _():
        total[...] += part

    @pl.when(step == 3)
    def _():
        core, yl, yh = lax.axis_index("core"), lax.axis_index("yl"), lax.axis_index("yh")
        before = [prev_ref[f].reshape(64, 64) for f in range(2)]
        total[0] += jnp.concatenate(before, axis=1)

        def joined(ref):
            halves = ref[...].astype(F32)
            halves = halves[0] + halves[1] + halves[2] + halves[3]
            return halves[:16] + halves[16:]

        mine, other = joined(mine_ref), joined(other_ref)
        share = jnp.concatenate(
            [jnp.where(core == 0, mine, other), jnp.where(core == 0, other, mine)], axis=0
        )
        for to in range(4):
            for half in range(2):
                d = (yh * 2 + yl + 4 - (half * 2 + to // 2)) % 4
                out_ref[to, half * 64 : half * 64 + 64] = total[d]
            out_ref[to, 128:] = share


def dots(s, pieces, half, extra=(), extra_specs=(), kernel=first_kernel, out=(256, 128), scratch=()):
    return pl.pallas_call(
        kernel,
        grid=(4,),
        in_specs=[pl.BlockSpec((1, 1056, 128), lambda i: (i, 0, 0))]
        + [pl.BlockSpec((1, 64, 1024), lambda i: (half * 4 + i, 0, 0))] * 4
        + list(extra_specs),
        out_specs=pl.BlockSpec(out, lambda i: (0,) * len(out)),
        out_shape=jax.ShapeDtypeStruct(out, F32),
        scratch_shapes=list(scratch),
        cost_estimate=pl.CostEstimate(
            flops=(1 << 28) if half else (30 << 30), bytes_accessed=3 << 20, transcendentals=0
        ),
        name=kernel.__name__,
    )(s, *pieces, *extra)


def last_kernel(in_ref, g_ref, s_ref):
    yh = lax.axis_index("yh")
    combined = in_ref[0, :128] + in_ref[1, :128] + in_ref[2, :128] + in_ref[3, :128]
    for f in range(2):
        share = in_ref[f, 128:] + in_ref[2 + f, 128:]
        rows = jnp.concatenate([share[:, :64], share[:, 64:]], axis=0)
        g = lax.dot_general(
            combined[:, f * 64 : f * 64 + 64],
            rows,
            (((1,), (1,)), ((), ())),
            precision=lax.Precision.HIGHEST,
            preferred_element_type=F32,
        )
        for r in range(2):
            low, high = g[r * 32 : r * 32 + 32], g[64 + r * 32 : 96 + r * 32]
            flipped = jnp.concatenate([low, high], axis=0).T
            mirror = jnp.where(yh == 0, flipped[:32], flipped[32:])
            mine = jnp.where(yh == 0, low, high)
            g_ref[f, r] = mine
            s_ref[f, r] = COUPLING * mine * mine * mirror


def body(g_hist, sigma_hist, diag_inv, previous, block_of_slot, front_pos):
    *pieces, share, chunk = prep(
        block_of_slot,
        front_pos,
        g_hist.reshape(64, 32768),
        sigma_hist.reshape(128, 128),
        diag_inv,
    )
    rows = [pieces[0]]
    for d in (2, 1, 3):
        pairs = [(ring_index(y), ring_index((y + d) % 4)) for y in range(4)]
        rows.append(lax.ppermute(pieces[d], RING, pairs))
    rows = [rows[0], rows[2], rows[1], rows[3]]
    shares = lax.all_gather(share, "core")
    message = pl.pallas_call(
        along_z_kernel,
        in_specs=[whole(), whole()],
        out_specs=whole(),
        out_shape=jax.ShapeDtypeStruct((16, 96, 128), BF16),
        name="along_z",
    )(shares, chunk)
    message = lax.all_to_all(message, "z", 0, 0, tiled=True)
    message = pl.pallas_call(
        along_x_kernel,
        in_specs=[whole()],
        out_specs=whole(),
        out_shape=jax.ShapeDtypeStruct((4, 1056, 128), BF16),
        name="along_x",
    )(message)
    mine = lax.all_to_all(message, "x", 0, 0, tiled=True)
    other = lax.ppermute(mine, "core", [(0, 1), (1, 0)])
    part = dots(mine, rows, 0)
    tail = pl.BlockSpec((4, SPLIT_ROWS, 128), lambda i: (0, 1024 // SPLIT_ROWS, 0))
    sums = dots(
        other,
        rows,
        1,
        (part.reshape(4, 64, 128), mine, other, previous),
        (
            pl.BlockSpec((4, 64, 128), lambda i: (0, 0, 0)),
            tail,
            tail,
            pl.BlockSpec((2, 2, 32, 64), lambda i: (0, 0, 0, 0)),
        ),
        second_kernel,
        (4, 160, 128),
        (VMEM((4, 64, 128), F32),),
    )
    sums = lax.all_to_all(sums, RING, 0, 0, tiled=True)
    out = jax.ShapeDtypeStruct(previous.shape, F32)
    return pl.pallas_call(
        last_kernel,
        in_specs=[whole()],
        out_specs=(whole(), whole()),
        out_shape=(out, out),
        name="last",
    )(sums)


def solution(mesh):
    split = Mesh(mesh.devices.reshape(16, 4, 2, 2, 2), (*HIST, "yh"))
    in_specs = (
        P(HIST, "yh", None),
        P(None, None, HIST),
        P(HIST, None, None),
        P(None, HIST, "yh", None),
        P(),
        P(),
    )
    out_specs = (P(None, HIST, "yh", None), P(None, HIST, "yh", None))
    return jax.shard_map(body, mesh=split, in_specs=in_specs, out_specs=out_specs, check_vma=False)
```

```python
import jax
import jax.numpy as jnp
from jax import lax
from jax.experimental import pallas as pl
from jax.experimental.pallas import tpu as pltpu
from jax.sharding import Mesh
from jax.sharding import PartitionSpec as P

HIST = ("z", "x", "yl", "core")
RING = ("yl", "yh")
COUPLING = 0.5
PAIRS = 4
SPLIT_ROWS = 32
F32 = jnp.float32
BF16 = jnp.bfloat16
VMEM = pltpu.VMEM
SMEM = pltpu.SMEM


ROOM = pltpu.CompilerParams(vmem_limit_bytes=20 << 20)


def whole(space=VMEM):
    return pl.BlockSpec(memory_space=space)


def near(value):
    return pltpu.with_memory_space_constraint(value, VMEM)


def far(value):
    return pltpu.with_memory_space_constraint(value, pltpu.HBM)


def ring_index(y):
    return (y % 2) * 2 + y // 2


def prep_kernel(slots, fronts, g_ref, sigma_ref, inv_ref, *outs):
    piece_refs, share_ref, chunk_ref = outs[:4], outs[4], outs[5]
    step = pl.program_id(0)
    yl, core, yh = lax.axis_index("yl"), lax.axis_index("core"), lax.axis_index("yh")
    hist = ((lax.axis_index("z") * 4 + lax.axis_index("x")) * 2 + yl) * 2 + core
    first = slots[hist] * 2
    lane = lax.broadcasted_iota(jnp.int32, (64, 128), 1)
    row = lax.broadcasted_iota(jnp.int32, (64, 128), 0)
    upper = (lane >= 64).astype(jnp.int32)
    ahead = upper * 32 - first - (row >= 32).astype(jnp.int32)
    pick_in = lax.broadcasted_iota(jnp.int32, (256, 256), 0)
    pick_out = lax.broadcasted_iota(jnp.int32, (256, 256), 1)
    for d in range(2):
        y = (yh * 2 + yl + d) % 4
        to_yl, to_yh = y % 2, y // 2
        half = jnp.where(pick_out < 128, to_yh, 1 - to_yh)
        within = pick_out % 128
        pick = pick_in == within + 64 * (within >= 64).astype(jnp.int32) + 64 * half
        pick = jnp.where(pick, 1.0, 0.0).astype(BF16)
        for p in range(PAIRS):
            blocks = []
            for h in range(2):
                to_core = core if h == 0 else 1 - core
                for x in range(4):
                    at = p * 4096 + (x * 4 + to_yl * 2 + to_core) * 128
                    even = g_ref[:, pl.ds(pl.multiple_of(at, 128), 128)]
                    odd = g_ref[:, pl.ds(pl.multiple_of(at + 2048, 128), 128)]
                    blocks.append(jnp.concatenate([even, odd], axis=1))
            picked = jnp.dot(jnp.concatenate(blocks, axis=0), pick, preferred_element_type=F32)
            for h in range(2):
                to_core = core if h == 0 else 1 - core
                for x in range(4):
                    at = h * 4 + x
                    term = (step * PAIRS + p) * 64 + x * 8 + to_yl * 4 + to_core * 2
                    for far in range(2):
                        e = 1 - to_yh if far else to_yh
                        block = picked[at * 64 : at * 64 + 64, far * 128 : far * 128 + 128]
                        block = jnp.where(ahead + (term + e) >= 0, block, 0.0)
                        piece_refs[d + 2 * far][at, :, p * 128 : p * 128 + 128] = block.astype(BF16)

    @pl.when(step == 0)
    def _():
        flipped = sigma_ref[...].astype(F32).T
        mine = jnp.where(yh == 0, flipped[:64], flipped[64:])
        limit = jnp.where(upper > 0, fronts[1], fronts[0])
        chunk_ref[...] = jnp.where(2 * hist + yh <= limit, mine, 0.0).astype(BF16)
        when = jnp.where(yh == 0, fronts[0], fronts[1])
        block = jnp.where(when % 2 == 0, inv_ref[0], inv_ref[1])
        block = jnp.where(when // 2 == hist, block, 0.0)
        share_ref[:, :64] = block[:32]
        share_ref[:, 64:] = block[32:]


def prep(slots, fronts, g_hist, sigma_hist, diag_inv):
    return pl.pallas_call(
        prep_kernel,
        grid=(8 // PAIRS,),
        in_specs=[
            whole(SMEM),
            whole(SMEM),
            pl.BlockSpec((64, 4096 * PAIRS), lambda i: (0, i)),
            pl.BlockSpec((128, 128), lambda i: (0, 0)),
            pl.BlockSpec((2, 64, 64), lambda i: (0, 0, 0)),
        ],
        out_specs=[pl.BlockSpec((8, 64, 128 * PAIRS), lambda i: (0, 0, i))] * 4
        + [pl.BlockSpec((32, 128), lambda i: (0, 0)), pl.BlockSpec((64, 128), lambda i: (0, 0))],
        out_shape=[pltpu.HBM((8, 64, 1024), BF16)] * 4
        + [VMEM((32, 128), F32), VMEM((64, 128), BF16)],
        compiler_params=ROOM,
        name="prep",
    )(far(slots), far(fronts), far(g_hist), far(sigma_hist), far(diag_inv))


def along_z_kernel(shares_ref, chunk_ref, out_ref):
    core = lax.axis_index("core")
    share = shares_ref[0] + shares_ref[1]
    mine = jnp.where(core == 0, share[:16], share[16:])
    high = mine.astype(BF16)
    low = (mine - high.astype(F32)).astype(BF16)
    message = jnp.concatenate([chunk_ref[...], high, low], axis=0)
    for z in range(16):
        out_ref[z] = message


def along_x_kernel(in_ref, out_ref):
    share = in_ref[0, 64:].astype(F32)
    for z in range(1, 16):
        share = share + in_ref[z, 64:].astype(F32)
    share = share.astype(BF16)
    for x in range(4):
        for z in range(16):
            out_ref[x, z * 64 : z * 64 + 64] = in_ref[z, :64]
        out_ref[x, 1024:] = share


def first_kernel(s_ref, g0, g1, g2, g3, out_ref):
    rows = jnp.concatenate([g0[0], g1[0], g2[0], g3[0]], axis=0)
    part = jnp.dot(rows, s_ref[0, :1024], preferred_element_type=F32)

    @pl.when(pl.program_id(0) == 0)
    def _():
        out_ref[...] = part

    @pl.when(pl.program_id(0) > 0)
    def _():
        out_ref[...] += part


def second_kernel(s_ref, g0, g1, g2, g3, part_ref, mine_ref, other_ref, prev_ref, out_ref, total):
    rows = jnp.concatenate([g0[0], g1[0], g2[0], g3[0]], axis=0)
    part = jnp.dot(rows, s_ref[0, :1024], preferred_element_type=F32).reshape(4, 64, 128)
    step = pl.program_id(0)

    @pl.when(step == 0)
    def _():
        total[...] = part + part_ref[...]

    @pl.when(step > 0)
    def _():
        total[...] += part

    @pl.when(step == 3)
    def _():
        core, yl, yh = lax.axis_index("core"), lax.axis_index("yl"), lax.axis_index("yh")
        before = [prev_ref[f].reshape(64, 64) for f in range(2)]
        total[0] += jnp.concatenate(before, axis=1)

        def joined(ref):
            halves = ref[...].astype(F32)
            halves = halves[0] + halves[1] + halves[2] + halves[3]
            return halves[:16] + halves[16:]

        mine, other = joined(mine_ref), joined(other_ref)
        share = jnp.concatenate(
            [jnp.where(core == 0, mine, other), jnp.where(core == 0, other, mine)], axis=0
        )
        for to in range(4):
            for half in range(2):
                d = (yh * 2 + yl + 4 - (half * 2 + to // 2)) % 4
                out_ref[to, half * 64 : half * 64 + 64] = total[d]
            out_ref[to, 128:] = share


def dots(s, pieces, half, extra=(), extra_specs=(), kernel=first_kernel, out=(256, 128), scratch=()):
    return pl.pallas_call(
        kernel,
        grid=(4,),
        in_specs=[pl.BlockSpec((1, 1056, 128), lambda i: (i, 0, 0))]
        + [pl.BlockSpec((1, 64, 1024), lambda i: (half * 4 + i, 0, 0))] * 4
        + list(extra_specs),
        out_specs=pl.BlockSpec(out, lambda i: (0,) * len(out)),
        out_shape=VMEM(out, F32),
        scratch_shapes=list(scratch),
        cost_estimate=pl.CostEstimate(
            flops=(1 << 28) if half else (30 << 30), bytes_accessed=3 << 20, transcendentals=0
        ),
        compiler_params=ROOM,
        name=kernel.__name__,
    )(near(s), *pieces, *[near(value) for value in extra])


def last_kernel(in_ref, g_ref, s_ref):
    yh = lax.axis_index("yh")
    combined = in_ref[0, :128] + in_ref[1, :128] + in_ref[2, :128] + in_ref[3, :128]
    for f in range(2):
        share = in_ref[f, 128:] + in_ref[2 + f, 128:]
        rows = jnp.concatenate([share[:, :64], share[:, 64:]], axis=0)
        g = lax.dot_general(
            combined[:, f * 64 : f * 64 + 64],
            rows,
            (((1,), (1,)), ((), ())),
            precision=lax.Precision.HIGHEST,
            preferred_element_type=F32,
        )
        for r in range(2):
            low, high = g[r * 32 : r * 32 + 32], g[64 + r * 32 : 96 + r * 32]
            flipped = jnp.concatenate([low, high], axis=0).T
            mirror = jnp.where(yh == 0, flipped[:32], flipped[32:])
            mine = jnp.where(yh == 0, low, high)
            g_ref[f, r] = mine
            s_ref[f, r] = COUPLING * mine * mine * mirror


def along_ring(piece, d):
    return lax.ppermute(piece, RING, [(ring_index(y), ring_index((y + d) % 4)) for y in range(4)])


def gathered(share, chunk, first, third):
    shares = lax.all_gather(share, "core")
    message = pl.pallas_call(
        along_z_kernel,
        in_specs=[whole(), whole()],
        out_specs=whole(),
        out_shape=VMEM((16, 96, 128), BF16),
        compiler_params=ROOM,
        name="along_z",
    )(near(shares), near(chunk))
    message = lax.all_to_all(message, "z", 0, 0, tiled=True)
    message = pl.pallas_call(
        along_x_kernel,
        in_specs=[whole()],
        out_specs=whole(),
        out_shape=VMEM((4, 1056, 128), BF16),
        compiler_params=ROOM,
        name="along_x",
    )(near(message))
    first, third = along_ring(first, 1), along_ring(third, 3)
    return lax.all_to_all(message, "x", 0, 0, tiled=True), first, third


def body(g_hist, sigma_hist, diag_inv, previous, block_of_slot, front_pos):
    *pieces, share, chunk = prep(
        block_of_slot,
        front_pos,
        g_hist.reshape(64, 32768),
        sigma_hist.reshape(128, 128),
        diag_inv,
    )
    opposite = along_ring(pieces[2], 2)
    mine, before, after = lax.cond(
        front_pos[0] >= 0,
        gathered,
        lambda share, chunk, *near_pieces: (jnp.zeros((4, 1056, 128), BF16), *near_pieces),
        share,
        chunk,
        pieces[1],
        pieces[3],
    )
    rows = [pieces[0], before, opposite, after]
    other = lax.ppermute(mine, "core", [(0, 1), (1, 0)])
    part = dots(mine, rows, 0)
    tail = pl.BlockSpec((4, SPLIT_ROWS, 128), lambda i: (0, 1024 // SPLIT_ROWS, 0))
    sums = dots(
        other,
        rows,
        1,
        (part.reshape(4, 64, 128), mine, other, previous),
        (
            pl.BlockSpec((4, 64, 128), lambda i: (0, 0, 0)),
            tail,
            tail,
            pl.BlockSpec((2, 2, 32, 64), lambda i: (0, 0, 0, 0)),
        ),
        second_kernel,
        (4, 160, 128),
        (VMEM((4, 64, 128), F32),),
    )
    sums = lax.all_to_all(sums, RING, 0, 0, tiled=True)
    out = jax.ShapeDtypeStruct(previous.shape, F32)
    return pl.pallas_call(
        last_kernel,
        in_specs=[whole()],
        out_specs=(whole(), whole()),
        out_shape=(out, out),
        compiler_params=ROOM,
        name="last",
    )(near(sums))


def solution(mesh):
    split = Mesh(mesh.devices.reshape(16, 4, 2, 2, 2), (*HIST, "yh"))
    in_specs = (
        P(HIST, "yh", None),
        P(None, None, HIST),
        P(HIST, None, None),
        P(None, HIST, "yh", None),
        P(),
        P(),
    )
    out_specs = (P(None, HIST, "yh", None), P(None, HIST, "yh", None))
    return jax.shard_map(body, mesh=split, in_specs=in_specs, out_specs=out_specs, check_vma=False)
```

```python
import jax
import jax.numpy as jnp
from jax import lax
from jax.experimental import pallas as pl
from jax.experimental.pallas import tpu as pltpu
from jax.sharding import Mesh
from jax.sharding import PartitionSpec as P

HIST = ("z", "x", "yl", "core")
RING = ("yl", "yh")
COUPLING = 0.5
PAIRS = 4
SPLIT_ROWS = 32
F32 = jnp.float32
BF16 = jnp.bfloat16
VMEM = pltpu.VMEM
SMEM = pltpu.SMEM


ROOM = pltpu.CompilerParams(vmem_limit_bytes=20 << 20)


def whole(space=VMEM):
    return pl.BlockSpec(memory_space=space)


def near(value):
    return pltpu.with_memory_space_constraint(value, VMEM)


def far(value):
    return pltpu.with_memory_space_constraint(value, pltpu.HBM)


def ring_index(y):
    return (y % 2) * 2 + y // 2


def sort_pieces(slots, g_ref, near_refs, far_refs):
    step = pl.program_id(0)
    yl, core, yh = lax.axis_index("yl"), lax.axis_index("core"), lax.axis_index("yh")
    hist = ((lax.axis_index("z") * 4 + lax.axis_index("x")) * 2 + yl) * 2 + core
    first = slots[hist] * 2
    lane = lax.broadcasted_iota(jnp.int32, (64, 128), 1)
    row = lax.broadcasted_iota(jnp.int32, (64, 128), 0)
    upper = (lane >= 64).astype(jnp.int32)
    ahead = upper * 32 - first - (row >= 32).astype(jnp.int32)
    for d, refs in enumerate(zip(near_refs, far_refs, strict=True)):
        y = (yh * 2 + yl + d) % 4
        to_yl = y % 2
        ends = [(ref, y // 2 if far == 0 else 1 - y // 2) for far, ref in enumerate(refs) if ref is not None]
        if not ends:
            continue
        width = 128 * len(ends)
        pick_in = lax.broadcasted_iota(jnp.int32, (256, width), 0)
        pick_out = lax.broadcasted_iota(jnp.int32, (256, width), 1)
        half = jnp.where(pick_out < 128, ends[0][1], ends[-1][1])
        within = pick_out % 128
        pick = pick_in == within + 64 * (within >= 64).astype(jnp.int32) + 64 * half
        pick = jnp.where(pick, 1.0, 0.0).astype(BF16)
        for p in range(PAIRS):
            blocks = []
            for h in range(2):
                to_core = core if h == 0 else 1 - core
                for x in range(4):
                    at = p * 4096 + (x * 4 + to_yl * 2 + to_core) * 128
                    even = g_ref[:, pl.ds(pl.multiple_of(at, 128), 128)]
                    odd = g_ref[:, pl.ds(pl.multiple_of(at + 2048, 128), 128)]
                    blocks.append(jnp.concatenate([even, odd], axis=1))
            picked = jnp.dot(jnp.concatenate(blocks, axis=0), pick, preferred_element_type=F32)
            for h in range(2):
                to_core = core if h == 0 else 1 - core
                for x in range(4):
                    at = h * 4 + x
                    term = (step * PAIRS + p) * 64 + x * 8 + to_yl * 4 + to_core * 2
                    for n, (ref, e) in enumerate(ends):
                        block = picked[at * 64 : at * 64 + 64, n * 128 : n * 128 + 128]
                        block = jnp.where(ahead + (term + e) >= 0, block, 0.0)
                        ref[at, :, p * 128 : p * 128 + 128] = block.astype(BF16)


def opposite_kernel(slots, fronts, g_ref, sigma_ref, inv_ref, piece_ref, share_ref, chunk_ref):
    sort_pieces(slots, g_ref, (None,), (piece_ref,))

    @pl.when(pl.program_id(0) == 0)
    def _():
        yh = lax.axis_index("yh")
        hist = 0
        for axis, size in zip(HIST, (16, 4, 2, 2), strict=True):
            hist = hist * size + lax.axis_index(axis)
        lane = lax.broadcasted_iota(jnp.int32, (64, 128), 1)
        flipped = sigma_ref[...].astype(F32).T
        mine = jnp.where(yh == 0, flipped[:64], flipped[64:])
        limit = jnp.where(lane >= 64, fronts[1], fronts[0])
        chunk_ref[...] = jnp.where(2 * hist + yh <= limit, mine, 0.0).astype(BF16)
        when = jnp.where(yh == 0, fronts[0], fronts[1])
        block = jnp.where(when % 2 == 0, inv_ref[0], inv_ref[1])
        block = jnp.where(when // 2 == hist, block, 0.0)
        share_ref[:, :64] = block[:32]
        share_ref[:, 64:] = block[32:]


def others_kernel(slots, g_ref, own_ref, first_ref, third_ref):
    sort_pieces(slots, g_ref, (own_ref, first_ref), (None, third_ref))


G_SPEC = pl.BlockSpec((64, 4096 * PAIRS), lambda i: (0, i))
PIECE_SPEC = pl.BlockSpec((8, 64, 128 * PAIRS), lambda i: (0, 0, i))
PIECE = pltpu.HBM((8, 64, 1024), BF16)


def prep_opposite(slots, fronts, g_hist, sigma_hist, diag_inv):
    return pl.pallas_call(
        opposite_kernel,
        grid=(8 // PAIRS,),
        in_specs=[
            whole(SMEM),
            whole(SMEM),
            G_SPEC,
            pl.BlockSpec((128, 128), lambda i: (0, 0)),
            pl.BlockSpec((2, 64, 64), lambda i: (0, 0, 0)),
        ],
        out_specs=[PIECE_SPEC]
        + [pl.BlockSpec((32, 128), lambda i: (0, 0)), pl.BlockSpec((64, 128), lambda i: (0, 0))],
        out_shape=[PIECE] + [VMEM((32, 128), F32), VMEM((64, 128), BF16)],
        compiler_params=ROOM,
        name="prep_opposite",
    )(far(slots), far(fronts), far(g_hist), far(sigma_hist), far(diag_inv))


def prep_others(slots, g_hist):
    return pl.pallas_call(
        others_kernel,
        grid=(8 // PAIRS,),
        in_specs=[whole(SMEM), G_SPEC],
        out_specs=[PIECE_SPEC] * 3,
        out_shape=[PIECE] * 3,
        compiler_params=ROOM,
        cost_estimate=pl.CostEstimate(flops=1 << 29, bytes_accessed=6 << 20, transcendentals=0),
        name="prep_others",
    )(far(slots), far(g_hist))


def along_z_kernel(shares_ref, chunk_ref, out_ref):
    core = lax.axis_index("core")
    share = shares_ref[0] + shares_ref[1]
    mine = jnp.where(core == 0, share[:16], share[16:])
    high = mine.astype(BF16)
    low = (mine - high.astype(F32)).astype(BF16)
    message = jnp.concatenate([chunk_ref[...], high, low], axis=0)
    for z in range(16):
        out_ref[z] = message


def along_x_kernel(in_ref, out_ref):
    share = in_ref[0, 64:].astype(F32)
    for z in range(1, 16):
        share = share + in_ref[z, 64:].astype(F32)
    share = share.astype(BF16)
    for x in range(4):
        for z in range(16):
            out_ref[x, z * 64 : z * 64 + 64] = in_ref[z, :64]
        out_ref[x, 1024:] = share


def first_kernel(s_ref, g0, g1, g2, g3, out_ref):
    rows = jnp.concatenate([g0[0], g1[0], g2[0], g3[0]], axis=0)
    part = jnp.dot(rows, s_ref[0, :1024], preferred_element_type=F32)

    @pl.when(pl.program_id(0) == 0)
    def _():
        out_ref[...] = part

    @pl.when(pl.program_id(0) > 0)
    def _():
        out_ref[...] += part


def second_kernel(s_ref, g0, g1, g2, g3, part_ref, mine_ref, other_ref, prev_ref, out_ref, total):
    rows = jnp.concatenate([g0[0], g1[0], g2[0], g3[0]], axis=0)
    part = jnp.dot(rows, s_ref[0, :1024], preferred_element_type=F32).reshape(4, 64, 128)
    step = pl.program_id(0)

    @pl.when(step == 0)
    def _():
        total[...] = part + part_ref[...]

    @pl.when(step > 0)
    def _():
        total[...] += part

    @pl.when(step == 3)
    def _():
        core, yl, yh = lax.axis_index("core"), lax.axis_index("yl"), lax.axis_index("yh")
        before = [prev_ref[f].reshape(64, 64) for f in range(2)]
        total[0] += jnp.concatenate(before, axis=1)

        def joined(ref):
            halves = ref[...].astype(F32)
            halves = halves[0] + halves[1] + halves[2] + halves[3]
            return halves[:16] + halves[16:]

        mine, other = joined(mine_ref), joined(other_ref)
        share = jnp.concatenate(
            [jnp.where(core == 0, mine, other), jnp.where(core == 0, other, mine)], axis=0
        )
        for to in range(4):
            for half in range(2):
                d = (yh * 2 + yl + 4 - (half * 2 + to // 2)) % 4
                out_ref[to, half * 64 : half * 64 + 64] = total[d]
            out_ref[to, 128:] = share


def dots(s, pieces, half, extra=(), extra_specs=(), kernel=first_kernel, out=(256, 128), scratch=()):
    return pl.pallas_call(
        kernel,
        grid=(4,),
        in_specs=[pl.BlockSpec((1, 1056, 128), lambda i: (i, 0, 0))]
        + [pl.BlockSpec((1, 64, 1024), lambda i: (half * 4 + i, 0, 0))] * 4
        + list(extra_specs),
        out_specs=pl.BlockSpec(out, lambda i: (0,) * len(out)),
        out_shape=VMEM(out, F32),
        scratch_shapes=list(scratch),
        cost_estimate=pl.CostEstimate(
            flops=(1 << 28) if half else (30 << 30), bytes_accessed=3 << 20, transcendentals=0
        ),
        compiler_params=ROOM,
        name=kernel.__name__,
    )(near(s), *pieces, *[near(value) for value in extra])


def last_kernel(in_ref, g_ref, s_ref):
    yh = lax.axis_index("yh")
    combined = in_ref[0, :128] + in_ref[1, :128] + in_ref[2, :128] + in_ref[3, :128]
    for f in range(2):
        share = in_ref[f, 128:] + in_ref[2 + f, 128:]
        rows = jnp.concatenate([share[:, :64], share[:, 64:]], axis=0)
        g = lax.dot_general(
            combined[:, f * 64 : f * 64 + 64],
            rows,
            (((1,), (1,)), ((), ())),
            precision=lax.Precision.HIGHEST,
            preferred_element_type=F32,
        )
        for r in range(2):
            low, high = g[r * 32 : r * 32 + 32], g[64 + r * 32 : 96 + r * 32]
            flipped = jnp.concatenate([low, high], axis=0).T
            mirror = jnp.where(yh == 0, flipped[:32], flipped[32:])
            mine = jnp.where(yh == 0, low, high)
            g_ref[f, r] = mine
            s_ref[f, r] = COUPLING * mine * mine * mirror


def along_ring(piece, d):
    return lax.ppermute(piece, RING, [(ring_index(y), ring_index((y + d) % 4)) for y in range(4)])


def gathered(share, chunk, slots, g_hist):
    own, first, third = prep_others(slots, g_hist)
    first, third = along_ring(first, 1), along_ring(third, 3)
    shares = lax.all_gather(share, "core")
    message = pl.pallas_call(
        along_z_kernel,
        in_specs=[whole(), whole()],
        out_specs=whole(),
        out_shape=VMEM((16, 96, 128), BF16),
        compiler_params=ROOM,
        name="along_z",
    )(near(shares), near(chunk))
    message = lax.all_to_all(message, "z", 0, 0, tiled=True)
    message = pl.pallas_call(
        along_x_kernel,
        in_specs=[whole()],
        out_specs=whole(),
        out_shape=VMEM((4, 1056, 128), BF16),
        compiler_params=ROOM,
        name="along_x",
    )(near(message))
    return lax.all_to_all(message, "x", 0, 0, tiled=True), own, first, third


def body(g_hist, sigma_hist, diag_inv, previous, block_of_slot, front_pos):
    g_hist = g_hist.reshape(64, 32768)
    opposite, share, chunk = prep_opposite(
        block_of_slot, front_pos, g_hist, sigma_hist.reshape(128, 128), diag_inv
    )
    opposite = along_ring(opposite, 2)
    mine, own, before, after = lax.cond(
        front_pos[0] >= 0,
        gathered,
        lambda *_: tuple(jnp.zeros(n, BF16) for n in ((4, 1056, 128), *[opposite.shape] * 3)),
        share,
        chunk,
        block_of_slot,
        g_hist,
    )
    rows = [own, before, opposite, after]
    other = lax.ppermute(mine, "core", [(0, 1), (1, 0)])
    part = dots(mine, rows, 0)
    tail = pl.BlockSpec((4, SPLIT_ROWS, 128), lambda i: (0, 1024 // SPLIT_ROWS, 0))
    sums = dots(
        other,
        rows,
        1,
        (part.reshape(4, 64, 128), mine, other, previous),
        (
            pl.BlockSpec((4, 64, 128), lambda i: (0, 0, 0)),
            tail,
            tail,
            pl.BlockSpec((2, 2, 32, 64), lambda i: (0, 0, 0, 0)),
        ),
        second_kernel,
        (4, 160, 128),
        (VMEM((4, 64, 128), F32),),
    )
    sums = lax.all_to_all(sums, RING, 0, 0, tiled=True)
    out = jax.ShapeDtypeStruct(previous.shape, F32)
    return pl.pallas_call(
        last_kernel,
        in_specs=[whole()],
        out_specs=(whole(), whole()),
        out_shape=(out, out),
        compiler_params=ROOM,
        name="last",
    )(near(sums))


def solution(mesh):
    split = Mesh(mesh.devices.reshape(16, 4, 2, 2, 2), (*HIST, "yh"))
    in_specs = (
        P(HIST, "yh", None),
        P(None, None, HIST),
        P(HIST, None, None),
        P(None, HIST, "yh", None),
        P(),
        P(),
    )
    out_specs = (P(None, HIST, "yh", None), P(None, HIST, "yh", None))
    return jax.shard_map(body, mesh=split, in_specs=in_specs, out_specs=out_specs, check_vma=False)
```

```python
import jax
import jax.numpy as jnp
from jax import lax
from jax.experimental import pallas as pl
from jax.experimental.pallas import tpu as pltpu
from jax.sharding import Mesh
from jax.sharding import PartitionSpec as P

HIST = ("z", "x", "yl", "core")
RING = ("yl", "yh")
COUPLING = 0.5
PAIRS = 4
SPLIT_ROWS = 32
F32 = jnp.float32
BF16 = jnp.bfloat16
VMEM = pltpu.VMEM
SMEM = pltpu.SMEM


ROOM = pltpu.CompilerParams(vmem_limit_bytes=20 << 20)


def whole(space=VMEM):
    return pl.BlockSpec(memory_space=space)


def near(value):
    return pltpu.with_memory_space_constraint(value, VMEM)


def far(value):
    return pltpu.with_memory_space_constraint(value, pltpu.HBM)


def ring_index(y):
    return (y % 2) * 2 + y // 2


def sort_pieces(slots, g_ref, near_refs, far_refs):
    step = pl.program_id(0)
    yl, core, yh = lax.axis_index("yl"), lax.axis_index("core"), lax.axis_index("yh")
    hist = ((lax.axis_index("z") * 4 + lax.axis_index("x")) * 2 + yl) * 2 + core
    first = slots[hist] * 2
    lane = lax.broadcasted_iota(jnp.int32, (64, 128), 1)
    row = lax.broadcasted_iota(jnp.int32, (64, 128), 0)
    upper = (lane >= 64).astype(jnp.int32)
    ahead = upper * 32 - first - (row >= 32).astype(jnp.int32)
    for d, refs in enumerate(zip(near_refs, far_refs, strict=True)):
        y = (yh * 2 + yl + d) % 4
        to_yl = y % 2
        ends = [(ref, y // 2 if far == 0 else 1 - y // 2) for far, ref in enumerate(refs) if ref is not None]
        if not ends:
            continue
        width = 128 * len(ends)
        pick_in = lax.broadcasted_iota(jnp.int32, (256, width), 0)
        pick_out = lax.broadcasted_iota(jnp.int32, (256, width), 1)
        half = jnp.where(pick_out < 128, ends[0][1], ends[-1][1])
        within = pick_out % 128
        pick = pick_in == within + 64 * (within >= 64).astype(jnp.int32) + 64 * half
        pick = jnp.where(pick, 1.0, 0.0).astype(BF16)
        for p in range(PAIRS):
            blocks = []
            for h in range(2):
                to_core = core if h == 0 else 1 - core
                for x in range(4):
                    at = p * 4096 + (x * 4 + to_yl * 2 + to_core) * 128
                    even = g_ref[:, pl.ds(pl.multiple_of(at, 128), 128)]
                    odd = g_ref[:, pl.ds(pl.multiple_of(at + 2048, 128), 128)]
                    blocks.append(jnp.concatenate([even, odd], axis=1))
            picked = jnp.dot(jnp.concatenate(blocks, axis=0), pick, preferred_element_type=F32)
            for h in range(2):
                to_core = core if h == 0 else 1 - core
                for x in range(4):
                    at = h * 4 + x
                    term = (step * PAIRS + p) * 64 + x * 8 + to_yl * 4 + to_core * 2
                    for n, (ref, e) in enumerate(ends):
                        block = picked[at * 64 : at * 64 + 64, n * 128 : n * 128 + 128]
                        block = jnp.where(ahead + (term + e) >= 0, block, 0.0)
                        ref[at, :, p * 128 : p * 128 + 128] = block.astype(BF16)


def opposite_kernel(slots, fronts, g_ref, sigma_ref, inv_ref, piece_ref, share_ref, chunk_ref):
    sort_pieces(slots, g_ref, (None,), (piece_ref,))

    @pl.when(pl.program_id(0) == 0)
    def _():
        yh = lax.axis_index("yh")
        hist = 0
        for axis, size in zip(HIST, (16, 4, 2, 2), strict=True):
            hist = hist * size + lax.axis_index(axis)
        lane = lax.broadcasted_iota(jnp.int32, (64, 128), 1)
        flipped = sigma_ref[...].astype(F32).T
        mine = jnp.where(yh == 0, flipped[:64], flipped[64:])
        limit = jnp.where(lane >= 64, fronts[1], fronts[0])
        chunk_ref[...] = jnp.where(2 * hist + yh <= limit, mine, 0.0).astype(BF16)
        when = jnp.where(yh == 0, fronts[0], fronts[1])
        block = jnp.where(when % 2 == 0, inv_ref[0], inv_ref[1])
        block = jnp.where(when // 2 == hist, block, 0.0)
        share_ref[:, :64] = block[:32]
        share_ref[:, 64:] = block[32:]


def others_kernel(slots, g_ref, own_ref, first_ref, third_ref):
    sort_pieces(slots, g_ref, (own_ref, first_ref), (None, third_ref))


G_SPEC = pl.BlockSpec((64, 4096 * PAIRS), lambda i: (0, i))
PIECE_SPEC = pl.BlockSpec((8, 64, 128 * PAIRS), lambda i: (0, 0, i))
PIECE = pltpu.HBM((8, 64, 1024), BF16)


def prep_opposite(slots, fronts, g_hist, sigma_hist, diag_inv):
    return pl.pallas_call(
        opposite_kernel,
        grid=(8 // PAIRS,),
        in_specs=[
            whole(SMEM),
            whole(SMEM),
            G_SPEC,
            pl.BlockSpec((128, 128), lambda i: (0, 0)),
            pl.BlockSpec((2, 64, 64), lambda i: (0, 0, 0)),
        ],
        out_specs=[PIECE_SPEC]
        + [pl.BlockSpec((32, 128), lambda i: (0, 0)), pl.BlockSpec((64, 128), lambda i: (0, 0))],
        out_shape=[PIECE] + [VMEM((32, 128), F32), VMEM((64, 128), BF16)],
        compiler_params=ROOM,
        name="prep_opposite",
    )(far(slots), far(fronts), far(g_hist), far(sigma_hist), far(diag_inv))


def prep_others(slots, g_hist):
    return pl.pallas_call(
        others_kernel,
        grid=(8 // PAIRS,),
        in_specs=[whole(SMEM), G_SPEC],
        out_specs=[PIECE_SPEC] * 3,
        out_shape=[PIECE] * 3,
        compiler_params=ROOM,
        cost_estimate=pl.CostEstimate(flops=1 << 29, bytes_accessed=6 << 20, transcendentals=0),
        name="prep_others",
    )(far(slots), far(g_hist))


def along_z_kernel(shares_ref, chunk_ref, out_ref):
    core = lax.axis_index("core")
    share = shares_ref[0] + shares_ref[1]
    mine = jnp.where(core == 0, share[:16], share[16:])
    high = mine.astype(BF16)
    low = (mine - high.astype(F32)).astype(BF16)
    message = jnp.concatenate([chunk_ref[...], high, low], axis=0)
    for z in range(16):
        out_ref[z] = message


def along_x_kernel(in_ref, out_ref):
    share = in_ref[0, 64:].astype(F32)
    for z in range(1, 16):
        share = share + in_ref[z, 64:].astype(F32)
    share = share.astype(BF16)
    for x in range(4):
        for z in range(16):
            out_ref[x, z * 64 : z * 64 + 64] = in_ref[z, :64]
        out_ref[x, 1024:] = share


def both_dots(s_ref, *pieces):
    part = jnp.zeros((256, 128), F32)
    for x in range(2):
        rows = jnp.concatenate([piece[x] for piece in pieces], axis=0)
        part = part + jnp.dot(rows, s_ref[x, :1024], preferred_element_type=F32)
    return part


def first_kernel(s_ref, g0, g1, g2, g3, out_ref):
    part = both_dots(s_ref, g0, g1, g2, g3)

    @pl.when(pl.program_id(0) == 0)
    def _():
        out_ref[...] = part

    @pl.when(pl.program_id(0) > 0)
    def _():
        out_ref[...] += part


def second_kernel(s_ref, g0, g1, g2, g3, part_ref, mine_ref, other_ref, prev_ref, out_ref, total):
    part = both_dots(s_ref, g0, g1, g2, g3).reshape(4, 64, 128)
    step = pl.program_id(0)

    @pl.when(step == 0)
    def _():
        total[...] = part + part_ref[...]

    @pl.when(step > 0)
    def _():
        total[...] += part

    @pl.when(step == 1)
    def _():
        core, yl, yh = lax.axis_index("core"), lax.axis_index("yl"), lax.axis_index("yh")
        before = [prev_ref[f].reshape(64, 64) for f in range(2)]
        total[0] += jnp.concatenate(before, axis=1)

        def joined(ref):
            halves = ref[...].astype(F32)
            halves = halves[0] + halves[1] + halves[2] + halves[3]
            return halves[:16] + halves[16:]

        mine, other = joined(mine_ref), joined(other_ref)
        share = jnp.concatenate(
            [jnp.where(core == 0, mine, other), jnp.where(core == 0, other, mine)], axis=0
        )
        for to in range(4):
            for half in range(2):
                d = (yh * 2 + yl + 4 - (half * 2 + to // 2)) % 4
                out_ref[to, half * 64 : half * 64 + 64] = total[d]
            out_ref[to, 128:] = share


def dots(s, pieces, half, extra=(), extra_specs=(), kernel=first_kernel, out=(256, 128), scratch=()):
    return pl.pallas_call(
        kernel,
        grid=(2,),
        in_specs=[pl.BlockSpec((2, 1056, 128), lambda i: (i, 0, 0))]
        + [pl.BlockSpec((2, 64, 1024), lambda i: (half * 2 + i, 0, 0))] * 4
        + list(extra_specs),
        out_specs=pl.BlockSpec(out, lambda i: (0,) * len(out)),
        out_shape=VMEM(out, F32),
        scratch_shapes=list(scratch),
        cost_estimate=pl.CostEstimate(
            flops=(1 << 28) if half else (30 << 30), bytes_accessed=3 << 20, transcendentals=0
        ),
        compiler_params=ROOM,
        name=kernel.__name__,
    )(near(s), *pieces, *[near(value) for value in extra])


def last_kernel(in_ref, g_ref, s_ref):
    yh = lax.axis_index("yh")
    combined = in_ref[0, :128] + in_ref[1, :128] + in_ref[2, :128] + in_ref[3, :128]
    for f in range(2):
        share = in_ref[f, 128:] + in_ref[2 + f, 128:]
        rows = jnp.concatenate([share[:, :64], share[:, 64:]], axis=0)
        g = lax.dot_general(
            combined[:, f * 64 : f * 64 + 64],
            rows,
            (((1,), (1,)), ((), ())),
            precision=lax.Precision.HIGHEST,
            preferred_element_type=F32,
        )
        for r in range(2):
            low, high = g[r * 32 : r * 32 + 32], g[64 + r * 32 : 96 + r * 32]
            flipped = jnp.concatenate([low, high], axis=0).T
            mirror = jnp.where(yh == 0, flipped[:32], flipped[32:])
            mine = jnp.where(yh == 0, low, high)
            g_ref[f, r] = mine
            s_ref[f, r] = COUPLING * mine * mine * mirror


def along_ring(piece, d):
    return lax.ppermute(piece, RING, [(ring_index(y), ring_index((y + d) % 4)) for y in range(4)])


def gathered(share, chunk, slots, g_hist):
    own, first, third = prep_others(slots, g_hist)
    first, third = along_ring(first, 1), along_ring(third, 3)
    shares = lax.all_gather(share, "core")
    message = pl.pallas_call(
        along_z_kernel,
        in_specs=[whole(), whole()],
        out_specs=whole(),
        out_shape=VMEM((16, 96, 128), BF16),
        compiler_params=ROOM,
        name="along_z",
    )(near(shares), near(chunk))
    message = lax.all_to_all(message, "z", 0, 0, tiled=True)
    message = pl.pallas_call(
        along_x_kernel,
        in_specs=[whole()],
        out_specs=whole(),
        out_shape=VMEM((4, 1056, 128), BF16),
        compiler_params=ROOM,
        name="along_x",
    )(near(message))
    return lax.all_to_all(message, "x", 0, 0, tiled=True), own, first, third


def body(g_hist, sigma_hist, diag_inv, previous, block_of_slot, front_pos):
    g_hist = g_hist.reshape(64, 32768)
    opposite, share, chunk = prep_opposite(
        block_of_slot, front_pos, g_hist, sigma_hist.reshape(128, 128), diag_inv
    )
    opposite = along_ring(opposite, 2)
    mine, own, before, after = lax.cond(
        front_pos[0] >= 0,
        gathered,
        lambda *_: tuple(jnp.zeros(n, BF16) for n in ((4, 1056, 128), *[opposite.shape] * 3)),
        share,
        chunk,
        block_of_slot,
        g_hist,
    )
    rows = [own, before, opposite, after]
    other = lax.ppermute(mine, "core", [(0, 1), (1, 0)])
    part = dots(mine, rows, 0)
    tail = pl.BlockSpec((4, SPLIT_ROWS, 128), lambda i: (0, 1024 // SPLIT_ROWS, 0))
    sums = dots(
        other,
        rows,
        1,
        (part.reshape(4, 64, 128), mine, other, previous),
        (
            pl.BlockSpec((4, 64, 128), lambda i: (0, 0, 0)),
            tail,
            tail,
            pl.BlockSpec((2, 2, 32, 64), lambda i: (0, 0, 0, 0)),
        ),
        second_kernel,
        (4, 160, 128),
        (VMEM((4, 64, 128), F32),),
    )
    sums = lax.all_to_all(sums, RING, 0, 0, tiled=True)
    out = jax.ShapeDtypeStruct(previous.shape, F32)
    return pl.pallas_call(
        last_kernel,
        in_specs=[whole()],
        out_specs=(whole(), whole()),
        out_shape=(out, out),
        compiler_params=ROOM,
        name="last",
    )(near(sums))


def solution(mesh):
    split = Mesh(mesh.devices.reshape(16, 4, 2, 2, 2), (*HIST, "yh"))
    in_specs = (
        P(HIST, "yh", None),
        P(None, None, HIST),
        P(HIST, None, None),
        P(None, HIST, "yh", None),
        P(),
        P(),
    )
    out_specs = (P(None, HIST, "yh", None), P(None, HIST, "yh", None))
    return jax.shard_map(body, mesh=split, in_specs=in_specs, out_specs=out_specs, check_vma=False)
```

```python
import jax
import jax.numpy as jnp
from jax import lax
from jax.experimental import pallas as pl
from jax.experimental.pallas import tpu as pltpu
from jax.sharding import Mesh
from jax.sharding import PartitionSpec as P

HIST = ("z", "x", "yl", "core")
RING = ("yl", "yh")
COUPLING = 0.5
PAIRS = 4
SPLIT_ROWS = 32
F32 = jnp.float32
BF16 = jnp.bfloat16
VMEM = pltpu.VMEM
SMEM = pltpu.SMEM


ROOM = pltpu.CompilerParams(vmem_limit_bytes=20 << 20)


def whole(space=VMEM):
    return pl.BlockSpec(memory_space=space)


def near(value):
    return pltpu.with_memory_space_constraint(value, VMEM)


def far(value):
    return pltpu.with_memory_space_constraint(value, pltpu.HBM)


def ring_index(y):
    return (y % 2) * 2 + y // 2


def sort_pieces(slots, g_ref, near_refs, far_refs):
    step = pl.program_id(0)
    yl, core, yh = lax.axis_index("yl"), lax.axis_index("core"), lax.axis_index("yh")
    hist = ((lax.axis_index("z") * 4 + lax.axis_index("x")) * 2 + yl) * 2 + core
    first = slots[hist] * 2
    lane = lax.broadcasted_iota(jnp.int32, (64, 128), 1)
    row = lax.broadcasted_iota(jnp.int32, (64, 128), 0)
    upper = (lane >= 64).astype(jnp.int32)
    ahead = upper * 32 - first - (row >= 32).astype(jnp.int32)
    for d, refs in enumerate(zip(near_refs, far_refs, strict=True)):
        y = (yh * 2 + yl + d) % 4
        to_yl = y % 2
        ends = [(ref, y // 2 if far == 0 else 1 - y // 2) for far, ref in enumerate(refs) if ref is not None]
        if not ends:
            continue
        width = 128 * len(ends)
        pick_in = lax.broadcasted_iota(jnp.int32, (256, width), 0)
        pick_out = lax.broadcasted_iota(jnp.int32, (256, width), 1)
        half = jnp.where(pick_out < 128, ends[0][1], ends[-1][1])
        within = pick_out % 128
        pick = pick_in == within + 64 * (within >= 64).astype(jnp.int32) + 64 * half
        pick = jnp.where(pick, 1.0, 0.0).astype(BF16)
        for p in range(PAIRS):
            blocks = []
            for h in range(2):
                to_core = core if h == 0 else 1 - core
                for x in range(4):
                    at = p * 4096 + (x * 4 + to_yl * 2 + to_core) * 128
                    even = g_ref[:, pl.ds(pl.multiple_of(at, 128), 128)]
                    odd = g_ref[:, pl.ds(pl.multiple_of(at + 2048, 128), 128)]
                    blocks.append(jnp.concatenate([even, odd], axis=1))
            picked = jnp.dot(jnp.concatenate(blocks, axis=0), pick, preferred_element_type=F32)
            for h in range(2):
                to_core = core if h == 0 else 1 - core
                for x in range(4):
                    at = h * 4 + x
                    term = (step * PAIRS + p) * 64 + x * 8 + to_yl * 4 + to_core * 2
                    for n, (ref, e) in enumerate(ends):
                        block = picked[at * 64 : at * 64 + 64, n * 128 : n * 128 + 128]
                        block = jnp.where(ahead + (term + e) >= 0, block, 0.0)
                        ref[at, :, p * 128 : p * 128 + 128] = block.astype(BF16)


def opposite_kernel(slots, fronts, g_ref, sigma_ref, inv_ref, piece_ref, share_ref, chunk_ref):
    sort_pieces(slots, g_ref, (None,), (piece_ref,))

    @pl.when(pl.program_id(0) == 0)
    def _():
        yh = lax.axis_index("yh")
        hist = 0
        for axis, size in zip(HIST, (16, 4, 2, 2), strict=True):
            hist = hist * size + lax.axis_index(axis)
        lane = lax.broadcasted_iota(jnp.int32, (64, 128), 1)
        flipped = sigma_ref[...].astype(F32).T
        mine = jnp.where(yh == 0, flipped[:64], flipped[64:])
        limit = jnp.where(lane >= 64, fronts[1], fronts[0])
        chunk_ref[...] = jnp.where(2 * hist + yh <= limit, mine, 0.0).astype(BF16)
        when = jnp.where(yh == 0, fronts[0], fronts[1])
        block = jnp.where(when % 2 == 0, inv_ref[0], inv_ref[1])
        block = jnp.where(when // 2 == hist, block, 0.0)
        share_ref[:, :64] = block[:32]
        share_ref[:, 64:] = block[32:]


def others_kernel(slots, g_ref, own_ref, first_ref, third_ref):
    sort_pieces(slots, g_ref, (own_ref, first_ref), (None, third_ref))


G_SPEC = pl.BlockSpec((64, 4096 * PAIRS), lambda i: (0, i))
PIECE_SPEC = pl.BlockSpec((8, 64, 128 * PAIRS), lambda i: (0, 0, i))
PIECE = pltpu.HBM((8, 64, 1024), BF16)


def prep_opposite(slots, fronts, g_hist, sigma_hist, diag_inv):
    return pl.pallas_call(
        opposite_kernel,
        grid=(8 // PAIRS,),
        in_specs=[
            whole(SMEM),
            whole(SMEM),
            G_SPEC,
            pl.BlockSpec((128, 128), lambda i: (0, 0)),
            pl.BlockSpec((2, 64, 64), lambda i: (0, 0, 0)),
        ],
        out_specs=[PIECE_SPEC]
        + [pl.BlockSpec((32, 128), lambda i: (0, 0)), pl.BlockSpec((64, 128), lambda i: (0, 0))],
        out_shape=[PIECE] + [VMEM((32, 128), F32), VMEM((64, 128), BF16)],
        compiler_params=ROOM,
        name="prep_opposite",
    )(far(slots), far(fronts), far(g_hist), far(sigma_hist), far(diag_inv))


def prep_others(slots, g_hist):
    return pl.pallas_call(
        others_kernel,
        grid=(8 // PAIRS,),
        in_specs=[whole(SMEM), G_SPEC],
        out_specs=[PIECE_SPEC] * 3,
        out_shape=[PIECE] * 3,
        compiler_params=ROOM,
        cost_estimate=pl.CostEstimate(flops=1 << 29, bytes_accessed=6 << 20, transcendentals=0),
        name="prep_others",
    )(far(slots), far(g_hist))


def along_z_kernel(shares_ref, chunk_ref, out_ref):
    core = lax.axis_index("core")
    share = shares_ref[0] + shares_ref[1]
    mine = jnp.where(core == 0, share[:16], share[16:])
    high = mine.astype(BF16)
    low = (mine - high.astype(F32)).astype(BF16)
    message = jnp.concatenate([chunk_ref[...], high, low], axis=0)
    for z in range(16):
        out_ref[z] = message


def along_x_kernel(in_ref, out_ref):
    share = in_ref[0, 64:].astype(F32)
    for z in range(1, 16):
        share = share + in_ref[z, 64:].astype(F32)
    share = share.astype(BF16)
    for x in range(4):
        for z in range(16):
            out_ref[x, z * 64 : z * 64 + 64] = in_ref[z, :64]
        out_ref[x, 1024:] = share


def both_dots(s_ref, *pieces):
    part = jnp.zeros((256, 128), F32)
    for x in range(4):
        rows = jnp.concatenate([piece[x] for piece in pieces], axis=0)
        part = part + jnp.dot(rows, s_ref[x, :1024], preferred_element_type=F32)
    return part


def first_kernel(s_ref, g0, g1, g2, g3, out_ref):
    part = both_dots(s_ref, g0, g1, g2, g3)

    @pl.when(pl.program_id(0) == 0)
    def _():
        out_ref[...] = part

    @pl.when(pl.program_id(0) > 0)
    def _():
        out_ref[...] += part


def second_kernel(s_ref, g0, g1, g2, g3, part_ref, mine_ref, other_ref, prev_ref, out_ref, total):
    part = both_dots(s_ref, g0, g1, g2, g3).reshape(4, 64, 128)
    step = pl.program_id(0)

    @pl.when(step == 0)
    def _():
        total[...] = part + part_ref[...]

    @pl.when(step > 0)
    def _():
        total[...] += part

    @pl.when(step == 0)
    def _():
        core, yl, yh = lax.axis_index("core"), lax.axis_index("yl"), lax.axis_index("yh")
        before = [prev_ref[f].reshape(64, 64) for f in range(2)]
        total[0] += jnp.concatenate(before, axis=1)

        def joined(ref):
            halves = ref[...].astype(F32)
            halves = halves[0] + halves[1] + halves[2] + halves[3]
            return halves[:16] + halves[16:]

        mine, other = joined(mine_ref), joined(other_ref)
        share = jnp.concatenate(
            [jnp.where(core == 0, mine, other), jnp.where(core == 0, other, mine)], axis=0
        )
        for to in range(4):
            for half in range(2):
                d = (yh * 2 + yl + 4 - (half * 2 + to // 2)) % 4
                out_ref[to, half * 64 : half * 64 + 64] = total[d]
            out_ref[to, 128:] = share


def dots(s, pieces, half, extra=(), extra_specs=(), kernel=first_kernel, out=(256, 128), scratch=()):
    return pl.pallas_call(
        kernel,
        grid=(1,),
        in_specs=[pl.BlockSpec((4, 1056, 128), lambda i: (i, 0, 0))]
        + [pl.BlockSpec((4, 64, 1024), lambda i: (half + i, 0, 0))] * 4
        + list(extra_specs),
        out_specs=pl.BlockSpec(out, lambda i: (0,) * len(out)),
        out_shape=VMEM(out, F32),
        scratch_shapes=list(scratch),
        cost_estimate=pl.CostEstimate(
            flops=(1 << 28) if half else (30 << 30), bytes_accessed=3 << 20, transcendentals=0
        ),
        compiler_params=ROOM,
        name=kernel.__name__,
    )(near(s), *pieces, *[near(value) for value in extra])


def last_kernel(in_ref, g_ref, s_ref):
    yh = lax.axis_index("yh")
    combined = in_ref[0, :128] + in_ref[1, :128] + in_ref[2, :128] + in_ref[3, :128]
    for f in range(2):
        share = in_ref[f, 128:] + in_ref[2 + f, 128:]
        rows = jnp.concatenate([share[:, :64], share[:, 64:]], axis=0)
        g = lax.dot_general(
            combined[:, f * 64 : f * 64 + 64],
            rows,
            (((1,), (1,)), ((), ())),
            precision=lax.Precision.HIGHEST,
            preferred_element_type=F32,
        )
        for r in range(2):
            low, high = g[r * 32 : r * 32 + 32], g[64 + r * 32 : 96 + r * 32]
            flipped = jnp.concatenate([low, high], axis=0).T
            mirror = jnp.where(yh == 0, flipped[:32], flipped[32:])
            mine = jnp.where(yh == 0, low, high)
            g_ref[f, r] = mine
            s_ref[f, r] = COUPLING * mine * mine * mirror


def along_ring(piece, d):
    return lax.ppermute(piece, RING, [(ring_index(y), ring_index((y + d) % 4)) for y in range(4)])


def gathered(share, chunk, slots, g_hist):
    own, first, third = prep_others(slots, g_hist)
    first, third = along_ring(first, 1), along_ring(third, 3)
    shares = lax.all_gather(share, "core")
    message = pl.pallas_call(
        along_z_kernel,
        in_specs=[whole(), whole()],
        out_specs=whole(),
        out_shape=VMEM((16, 96, 128), BF16),
        compiler_params=ROOM,
        name="along_z",
    )(near(shares), near(chunk))
    message = lax.all_to_all(message, "z", 0, 0, tiled=True)
    message = pl.pallas_call(
        along_x_kernel,
        in_specs=[whole()],
        out_specs=whole(),
        out_shape=VMEM((4, 1056, 128), BF16),
        compiler_params=ROOM,
        name="along_x",
    )(near(message))
    return lax.all_to_all(message, "x", 0, 0, tiled=True), own, first, third


def body(g_hist, sigma_hist, diag_inv, previous, block_of_slot, front_pos):
    g_hist = g_hist.reshape(64, 32768)
    opposite, share, chunk = prep_opposite(
        block_of_slot, front_pos, g_hist, sigma_hist.reshape(128, 128), diag_inv
    )
    opposite = along_ring(opposite, 2)
    mine, own, before, after = lax.cond(
        front_pos[0] >= 0,
        gathered,
        lambda *_: tuple(jnp.zeros(n, BF16) for n in ((4, 1056, 128), *[opposite.shape] * 3)),
        share,
        chunk,
        block_of_slot,
        g_hist,
    )
    rows = [own, before, opposite, after]
    other = lax.ppermute(mine, "core", [(0, 1), (1, 0)])
    part = dots(mine, rows, 0)
    tail = pl.BlockSpec((4, SPLIT_ROWS, 128), lambda i: (0, 1024 // SPLIT_ROWS, 0))
    sums = dots(
        other,
        rows,
        1,
        (part.reshape(4, 64, 128), mine, other, previous),
        (
            pl.BlockSpec((4, 64, 128), lambda i: (0, 0, 0)),
            tail,
            tail,
            pl.BlockSpec((2, 2, 32, 64), lambda i: (0, 0, 0, 0)),
        ),
        second_kernel,
        (4, 160, 128),
        (VMEM((4, 64, 128), F32),),
    )
    sums = lax.all_to_all(sums, RING, 0, 0, tiled=True)
    out = jax.ShapeDtypeStruct(previous.shape, F32)
    return pl.pallas_call(
        last_kernel,
        in_specs=[whole()],
        out_specs=(whole(), whole()),
        out_shape=(out, out),
        compiler_params=ROOM,
        name="last",
    )(near(sums))


def solution(mesh):
    split = Mesh(mesh.devices.reshape(16, 4, 2, 2, 2), (*HIST, "yh"))
    in_specs = (
        P(HIST, "yh", None),
        P(None, None, HIST),
        P(HIST, None, None),
        P(None, HIST, "yh", None),
        P(),
        P(),
    )
    out_specs = (P(None, HIST, "yh", None), P(None, HIST, "yh", None))
    return jax.shard_map(body, mesh=split, in_specs=in_specs, out_specs=out_specs, check_vma=False)
```
